32 devices in a mesh: slab: 4 (over y, x), tile: 8 (over z, core).
Axes of the slice: x: 2, y: 2, z: 4, core: 2. Of those that a mesh axis runs over, the one named last changes fastest.
Arguments:
- features: bfloat16 [65536, 128], P(('slab', 'tile')), may hold values from -6 to 6
- conv_weight: bfloat16 [27, 128, 128], replicated, may hold values from -0.15625 to 0.15625
- down_weight: bfloat16 [8, 128, 128], replicated, may hold values from -0.25 to 0.25
- coarse_grad: bfloat16 [16384, 128], P(('slab', 'tile')), may hold values from -6 to 6
- rulebook: int32 [27, 65536], P(None, ('slab', 'tile')), may hold values from 0 to 3072, as said below
- boundary_rows: int32 [128, 256], P(('slab', 'tile')), may hold values from 0 to 2047, as said below
- parent_code: int32 [65536], P(('slab', 'tile')), may hold values from 0 to 4096, as said below
Outputs:
- coarse: bfloat16 [16384, 128], P(('slab', 'tile'))
- input_grad: float32 [65536, 128], P(('slab', 'tile'))
- conv_grad: float32 [27, 128, 128], replicated
- down_grad: float32 [8, 128, 128], replicated
The draws below stay inside these ranges and needn't reach their ends.
Inputs may be any that keep to these rules, and one draw needn't show every extreme that they name: `rulebook`: each partition has some number of live blocks of 128 rows, at least one and fewer than 16, at its start; rows of the remaining blocks are dead. For a live row, the centre offset (13) reads the row itself; other entries read a live local row, a received row (2048 to 3071) or the empty row 3072. For each offset and each aligned block of 128 rows of a partition, all entries other than 3072 lie in one aligned block of 128 rows of the extended table. Every entry of a dead row is 3072. `boundary_rows`: entries are live rows of the partition; repeats may occur. `parent_code`: within a partition the live rows with one parent have distinct child positions, at most 4 per parent; the parents of the rows of local block b lie in coarse rows b * 32 to (b + 1) * 32 - 1; dead rows have the code 8 * 512.
All inputs are finite; a program needn't handle non-finite values.
Results may differ from the reference program's by a relative error of at most 0.02.
Values may be sent and summed in bfloat16 or wider, within the bound.
A program may use at most 64 MiB of HBM per device.

```python
import jax
import jax.numpy as jnp
from jax import lax

C = 128
C2 = 128
KVOL = 27
CHILD = 8
BLOCK = 128
NB = 16
ROWS = 2048
BRD = 256
RC = 512
N_SLAB = 4
N_TILE = 8
DEVICES = 32


def live_rows(key):
    blocks = jax.random.randint(jax.random.fold_in(key, 7), (DEVICES,), max(1, NB // 4), NB)
    return (blocks * BLOCK).astype(jnp.int32)


def draw_rulebook(key, part):
    row_count = NB * BLOCK
    empty_row = row_count + 4 * BRD
    live = live_rows(key)
    live_blocks = (live // BLOCK)[None, :, None]
    shape_blocks = (KVOL, DEVICES, NB)
    picker = jax.random.randint(jax.random.fold_in(key, 1), shape_blocks, 0, 10)
    local_block = jax.random.randint(jax.random.fold_in(key, 2), shape_blocks, 0, 1 << 20) % live_blocks
    far_block = NB + jax.random.randint(jax.random.fold_in(key, 3), shape_blocks, 0, NB // 2)
    source = jnp.where(picker < 6, local_block, far_block)
    shape = (KVOL, DEVICES, NB, BLOCK)
    inner_idx = jax.random.randint(jax.random.fold_in(key, 8), shape, 0, BLOCK)
    keeper = jax.random.randint(jax.random.fold_in(key, 9), shape, 0, 10)
    index = jnp.where(keeper < 6, source[:, :, :, None] * BLOCK + inner_idx, empty_row)
    place = jnp.arange(row_count, dtype=jnp.int32).reshape(1, 1, NB, BLOCK)
    centre = (jnp.arange(KVOL, dtype=jnp.int32) == KVOL // 2).reshape(KVOL, 1, 1, 1)
    index = jnp.where(centre, jnp.broadcast_to(place, shape), index)
    index = jnp.where(place < live.reshape(1, DEVICES, 1, 1), index, empty_row)
    return index.reshape(KVOL, DEVICES * row_count).astype(jnp.int32)


def draw_boundary_rows(key, part):
    live = live_rows(key)[:, None, None]
    picks = jax.random.randint(jax.random.fold_in(key, 6), (DEVICES, 4, BRD), 0, 1 << 20) % live
    return picks.reshape(DEVICES * 4, BRD).astype(jnp.int32)


def draw_parent_code(key, part):
    row_count = NB * BLOCK
    quarter = BLOCK // 4
    keys_all = jax.random.split(jax.random.fold_in(key, 4), DEVICES * NB)
    orders = jax.vmap(lambda key_one: jax.random.permutation(key_one, BLOCK))(keys_all).reshape(DEVICES, NB, BLOCK)
    coin = jax.random.randint(jax.random.fold_in(key, 5), (DEVICES, NB, BLOCK), 0, 2)
    inside = jnp.arange(BLOCK, dtype=jnp.int32)
    block_idx = jnp.arange(NB, dtype=jnp.int32)
    code_at = (block_idx[None, :, None] * quarter + (inside // 4)[None, None, :]) * 8 + 2 * (inside % 4)[None, None, :] + coin
    codes = jax.vmap(lambda order_one, code_one: jnp.zeros((BLOCK,), jnp.int32).at[order_one].set(code_one))(orders.reshape(DEVICES * NB, BLOCK), code_at.reshape(DEVICES * NB, BLOCK))
    codes = codes.reshape(DEVICES, row_count)
    position = jnp.arange(row_count, dtype=jnp.int32)
    live = live_rows(key)[:, None]
    codes = jnp.where(position[None, :] < live, codes, row_count // 4 * 8)
    return codes.reshape(DEVICES * row_count).astype(jnp.int32)


def block_scale(own_key, shape, cuts, smallest, high):
    def one(dim, blocks):
        heights = jax.random.uniform(jax.random.fold_in(jax.random.fold_in(own_key, 6), dim), (blocks,), jnp.float32, smallest / len(cuts), high / len(cuts))
        return jnp.repeat(jnp.exp(heights), shape[dim] // blocks).reshape((-1,) + (1,) * (len(shape) - dim - 1))

    gain = one(*cuts[0])
    for cut in cuts[1:]:
        gain = gain * one(*cut)
    return gain


def normal_values(stream_key, extent, width, bound, shards=(), kind=jnp.bfloat16):
    result = width * jax.random.normal(stream_key, extent, jnp.float32)
    if shards:
        result = result * block_scale(stream_key, extent, shards, -0.22, 0.18)
    return jnp.clip(result, -bound, bound).astype(kind)


def setup_inputs(seed: int = 0) -> dict:
    key_of = jax.random.split(jax.random.key(seed), 8)
    return {
        "features": normal_values(key_of[0], (DEVICES * ROWS, C), 1.0, 6.0, ((0, 32),)),
        "conv_weight": normal_values(key_of[1], (KVOL, C, C), (11 * C) ** -0.5, 0.15625),
        "down_weight": normal_values(key_of[2], (CHILD, C, C2), (4 * C) ** -0.5, 0.25),
        "coarse_grad": normal_values(key_of[3], (DEVICES * RC, C2), 1.0, 6.0, ((0, 32),)),
        "rulebook": draw_rulebook(jax.random.fold_in(key_of[7], 71), 0),
        "boundary_rows": draw_boundary_rows(jax.random.fold_in(key_of[7], 71), 0),
        "parent_code": draw_parent_code(jax.random.fold_in(key_of[7], 71), 0),
    }


def reference(features, conv_weight, down_weight, coarse_grad, rulebook, boundary_rows, parent_code):
    part_count = N_SLAB * N_TILE
    row_count = NB * BLOCK
    coarse_rows = row_count // 4
    empty_row = row_count + 4 * BRD
    feat_all = features.reshape(part_count, row_count, C)
    lists_all = boundary_rows.reshape(part_count, 4, BRD)
    sent_all = jax.vmap(lambda feat_one, list_one: feat_one[list_one])(feat_all, lists_all)
    sent_grid = sent_all.reshape(N_SLAB, N_TILE, 4, BRD, C)
    zero_slab = jnp.zeros((1, N_TILE, BRD, C), jnp.bfloat16)
    zero_tile = jnp.zeros((N_SLAB, 1, BRD, C), jnp.bfloat16)
    from_below = jnp.concatenate([zero_slab, sent_grid[:-1, :, 0]], axis=0)
    from_above = jnp.concatenate([sent_grid[1:, :, 1], zero_slab], axis=0)
    from_left = jnp.concatenate([zero_tile, sent_grid[:, :-1, 2]], axis=1)
    from_right = jnp.concatenate([sent_grid[:, 1:, 3], zero_tile], axis=1)
    received = jnp.stack([from_below, from_above, from_left, from_right], axis=2)
    received = received.reshape(part_count, 4 * BRD, C)
    book_all = rulebook.reshape(KVOL, part_count, row_count).transpose(1, 0, 2)
    code_all = parent_code.reshape(part_count, row_count)
    grad_all = coarse_grad.reshape(part_count, coarse_rows, C2)
    down_flat = down_weight.astype(jnp.float32).reshape(CHILD * C, C2)
    conv_float = conv_weight.astype(jnp.float32)

    def one_part(totals, item):
        feat_one, recv_one, book_one, code_one, grad_one = item
        extended = jnp.concatenate([feat_one, recv_one, jnp.zeros((1, C), jnp.bfloat16)], axis=0)
        gathered = extended[book_one].astype(jnp.float32)
        pre = jnp.einsum('krc,kcd->rd', gathered, conv_float)
        hidden = jnp.maximum(pre, 0.0).astype(jnp.bfloat16)
        parent = code_one // 8
        slot_idx = code_one % 8
        has_parent = parent < coarse_rows
        onehot = (slot_idx[:, None] == jnp.arange(CHILD, dtype=jnp.int32)[None, :]) & has_parent[:, None]
        spread = (hidden.astype(jnp.float32)[:, None, :] * onehot[:, :, None].astype(jnp.float32)).reshape(row_count, CHILD * C)
        terms = jnp.dot(spread, down_flat)
        coarse_one = jnp.zeros((coarse_rows + 1, C2), jnp.float32).at[parent].add(terms)[:coarse_rows]
        grad_ext = jnp.concatenate([grad_one, jnp.zeros((1, C2), jnp.bfloat16)], axis=0)
        grad_rows = grad_ext[parent].astype(jnp.float32)
        spread_grad = jnp.dot(grad_rows, down_flat.T).reshape(row_count, CHILD, C)
        hidden_grad = jnp.sum(spread_grad * onehot[:, :, None].astype(jnp.float32), axis=1)
        pre_grad = jnp.where(pre > 0, hidden_grad, 0.0).astype(jnp.bfloat16).astype(jnp.float32)
        down_part = jnp.dot(spread.T, grad_rows)
        conv_part = jnp.einsum('krc,rd->kcd', gathered, pre_grad)
        back = jnp.einsum('rd,kcd->krc', pre_grad, conv_float)
        ext_grad = jnp.zeros((empty_row + 1, C), jnp.float32).at[book_one].add(back)
        new_totals = (totals[0] + conv_part, totals[1] + down_part)
        return new_totals, (coarse_one.astype(jnp.bfloat16), ext_grad[:row_count], ext_grad[row_count:empty_row])

    start = (jnp.zeros((KVOL, C, C), jnp.float32), jnp.zeros((CHILD * C, C2), jnp.float32))
    totals, stacked = lax.scan(one_part, start, (feat_all, received, book_all, code_all, grad_all))
    coarse_all, local_grad, halo_grad = stacked
    halo_grid = halo_grad.reshape(N_SLAB, N_TILE, 4, BRD, C)
    zero_slab_f = jnp.zeros((1, N_TILE, BRD, C), jnp.float32)
    zero_tile_f = jnp.zeros((N_SLAB, 1, BRD, C), jnp.float32)
    back_zero = jnp.concatenate([halo_grid[1:, :, 0], zero_slab_f], axis=0)
    back_one = jnp.concatenate([zero_slab_f, halo_grid[:-1, :, 1]], axis=0)
    back_two = jnp.concatenate([halo_grid[:, 1:, 2], zero_tile_f], axis=1)
    back_three = jnp.concatenate([zero_tile_f, halo_grid[:, :-1, 3]], axis=1)
    returned = jnp.stack([back_zero, back_one, back_two, back_three], axis=2).reshape(part_count, 4 * BRD, C)
    input_grad = jax.vmap(lambda grad_one, list_one, ret_one: grad_one.at[list_one].add(ret_one))(local_grad, lists_all.reshape(part_count, 4 * BRD), returned)
    return (coarse_all.reshape(part_count * coarse_rows, C2), input_grad.reshape(part_count * row_count, C), totals[0], totals[1].reshape(CHILD, C, C2))
```

```python
import jax
import jax.numpy as jnp
from jax import lax
from jax.experimental import pallas as pl
from jax.experimental.pallas import tpu as pltpu
from jax.sharding import PartitionSpec as P

BLOCK = 128
F32 = jnp.float32
BF16 = jnp.bfloat16
LAST = (((1,), (1,)), ((), ()))
FIRST = (((0,), (0,)), ((), ()))


def dot(a, b):
    return jnp.dot(a, b, preferred_element_type=F32)


def hot(rows, index):
    return (lax.broadcasted_iota(jnp.int32, (rows, index.shape[1]), 0) == index).astype(BF16)


def main_kernel(
    src, table, wflat, weight, down, cgrad, book, code,
    coarse, ext_grad, conv_grad, down_grad,
    gathered, pre_grad, spread, children,
):
    kernels, blocks = book.shape[0], book.shape[1]
    childs, _, quarter, chans = spread.shape
    live = blocks - 1
    ext_grad[...] = jnp.zeros_like(ext_grad)
    children[...] = jnp.zeros_like(children)
    for s in range(childs):
        one = lax.dot_general(cgrad[...], down[s], LAST, preferred_element_type=F32)
        spread[s] = one.astype(BF16).reshape(blocks, quarter, chans)

    def pick(k, b):
        return hot(BLOCK, book[k, pl.ds(b, 1), :] - src[k, b] * BLOCK)

    def forward(b, carry):
        for k in range(kernels):
            got = dot(table[src[k, b]], pick(k, b))
            gathered[k * BLOCK : (k + 1) * BLOCK, :] = got.astype(BF16)
        pre = dot(wflat[...], gathered[...]).T
        hidden = jnp.maximum(pre, 0.0).astype(BF16)
        own = code[pl.ds(b, 1), :]
        place = (own % childs) * quarter + (own // childs - b * quarter)
        place = jnp.where(own // childs < blocks * quarter, place, -1)
        family = hot(childs * quarter, place)
        kids = dot(family, hidden).astype(BF16)
        children[:, b] = kids.reshape(childs, quarter, chans)
        share = spread[:, b].reshape(childs * quarter, chans)
        back = lax.dot_general(family, share, FIRST, preferred_element_type=F32)
        pre_grad[b] = jnp.where(pre > 0, back, 0.0).astype(BF16)
        return carry

    lax.fori_loop(0, live, forward, 0)

    coarse_total = jnp.zeros(coarse.shape, F32)
    for s in range(childs):
        kids = children[s].reshape(blocks * quarter, chans)
        coarse_total += dot(kids, down[s])
        down_grad[s] = lax.dot_general(kids, cgrad[...], FIRST, preferred_element_type=F32)
    coarse[...] = coarse_total.astype(BF16)

    def backward(k, carry):
        total = jnp.zeros(conv_grad.shape[1:], F32)
        for b in range(0, live, 2):
            group = range(b, min(b + 2, live))
            sums = [dot(pick(k, i), pre_grad[i]).astype(BF16) for i in group]
            sums = jnp.concatenate(sums, axis=0)
            total += dot(jnp.concatenate([table[src[k, i]] for i in group], axis=1), sums)
            terms = lax.dot_general(sums, weight[k], LAST, preferred_element_type=F32)
            for place, i in enumerate(group):
                ext_grad[src[k, i]] += terms[place * BLOCK : (place + 1) * BLOCK]
        conv_grad[k] = total
        return carry

    lax.fori_loop(0, kernels, backward, 0)


def add_kernel(base, lists, coming, out):
    blocks = base.shape[0]
    for n in range(blocks):
        out[n] = base[n] + dot(hot(BLOCK, lists[...] - n * BLOCK), coming[...])


def body(features, conv_weight, down_weight, coarse_grad, rulebook, boundary_rows, parent_code):
    rows, chans = features.shape
    coarse_rows, out_chans = coarse_grad.shape
    list_len = boundary_rows.shape[1]
    childs = down_weight.shape[0]
    kernels = conv_weight.shape[0]
    blocks = rows // BLOCK
    halo_blocks = 4 * list_len // BLOCK
    total_blocks = blocks + halo_blocks

    def shift(value, axis, step):
        size = lax.axis_size(axis)
        pairs = [(i, i + step) for i in range(size) if 0 <= i + step < size]
        return lax.ppermute(value, axis, pairs)

    outgoing = features[boundary_rows]
    received = jnp.stack(
        [
            shift(outgoing[0], "slab", 1),
            shift(outgoing[1], "slab", -1),
            shift(outgoing[2], "tile", 1),
            shift(outgoing[3], "tile", -1),
        ]
    )
    extended = jnp.concatenate([features, received.reshape(4 * list_len, chans)], axis=0)
    table = extended.reshape(total_blocks, BLOCK, chans).transpose(0, 2, 1)
    wflat = conv_weight.transpose(2, 0, 1).reshape(out_chans, kernels * chans)
    book = rulebook.reshape(kernels, blocks, BLOCK)
    src = jnp.minimum(jnp.min(book, axis=2) // BLOCK, total_blocks - 1)
    vmem = pl.BlockSpec(memory_space=pltpu.VMEM)
    coarse, ext_grad, conv_part, down_part = pl.pallas_call(
        main_kernel,
        out_shape=(
            jax.ShapeDtypeStruct((coarse_rows, out_chans), BF16),
            jax.ShapeDtypeStruct((total_blocks, BLOCK, chans), F32),
            jax.ShapeDtypeStruct(conv_weight.shape, F32),
            jax.ShapeDtypeStruct(down_weight.shape, F32),
        ),
        in_specs=[pl.BlockSpec(memory_space=pltpu.SMEM)] + [vmem] * 7,
        out_specs=(vmem,) * 4,
        scratch_shapes=[
            pltpu.VMEM((kernels * BLOCK, BLOCK), BF16),
            pltpu.VMEM((blocks, BLOCK, chans), BF16),
            pltpu.VMEM((childs, blocks, coarse_rows // blocks, chans), BF16),
            pltpu.VMEM((childs, blocks, coarse_rows // blocks, chans), BF16),
        ],
        compiler_params=pltpu.CompilerParams(vmem_limit_bytes=40 * 2**20),
        name="sparse_conv",
    )(
        src, table, wflat, conv_weight, down_weight, coarse_grad, book,
        parent_code.reshape(blocks, BLOCK),
    )
    halo = ext_grad[blocks:].reshape(4, list_len, chans).astype(BF16)
    returned = jnp.concatenate(
        [
            shift(halo[0], "slab", -1),
            shift(halo[1], "slab", 1),
            shift(halo[2], "tile", -1),
            shift(halo[3], "tile", 1),
        ]
    )
    input_grad = pl.pallas_call(
        add_kernel,
        out_shape=jax.ShapeDtypeStruct((blocks, BLOCK, chans), F32),
        in_specs=[vmem] * 3,
        out_specs=vmem,
        compiler_params=pltpu.CompilerParams(vmem_limit_bytes=32 * 2**20),
        name="add_returned",
    )(ext_grad[:blocks], boundary_rows.reshape(1, 4 * list_len), returned)
    conv_grad, down_grad = lax.psum((conv_part, down_part), ("slab", "tile"))
    return (coarse, input_grad.reshape(rows, chans), conv_grad, down_grad)


def solution(mesh):
    return jax.shard_map(
        body,
        mesh=mesh,
        in_specs=(
            P(("slab", "tile"), None),
            P(),
            P(),
            P(("slab", "tile"), None),
            P(None, ("slab", "tile")),
            P(("slab", "tile"), None),
            P(("slab", "tile")),
        ),
        out_specs=(P(("slab", "tile"), None), P(("slab", "tile"), None), P(), P()),
        check_vma=False,
    )
```

```python
import functools

import jax
import jax.numpy as jnp
from jax import lax
from jax.experimental import pallas as pl
from jax.experimental.pallas import tpu as pltpu
from jax.sharding import PartitionSpec as P

BLOCK = 128
F32 = jnp.float32
BF16 = jnp.bfloat16
LAST = (((1,), (1,)), ((), ()))
FIRST = (((0,), (0,)), ((), ()))
MESH = pl.DeviceIdType.MESH


def dot(a, b):
    return jnp.dot(a, b, preferred_element_type=F32)


def hot(rows, index):
    return (lax.broadcasted_iota(jnp.int32, (rows, index.shape[1]), 0) == index).astype(BF16)


def main_kernel(
    src, table, wflat, weight, down, cgrad, book, code,
    coarse, part, local_grad, halo_grad,
    ext_grad, gathered, pre_grad, spread, children,
):
    kernels, blocks = book.shape[0], book.shape[1]
    childs, _, quarter, chans = spread.shape
    live = blocks - 1
    ext_grad[...] = jnp.zeros_like(ext_grad)
    children[...] = jnp.zeros_like(children)
    for s in range(childs):
        one = lax.dot_general(cgrad[...], down[s], LAST, preferred_element_type=F32)
        spread[s] = one.astype(BF16).reshape(blocks, quarter, chans)

    def pick(k, b):
        return hot(BLOCK, book[k, pl.ds(b, 1), :] - src[k, b] * BLOCK)

    def forward(b, carry):
        for k in range(kernels):
            got = dot(table[src[k, b]], pick(k, b))
            gathered[k * BLOCK : (k + 1) * BLOCK, :] = got.astype(BF16)
        pre = dot(wflat[...], gathered[...]).T
        hidden = jnp.maximum(pre, 0.0).astype(BF16)
        own = code[pl.ds(b, 1), :]
        place = (own % childs) * quarter + (own // childs - b * quarter)
        place = jnp.where(own // childs < blocks * quarter, place, -1)
        family = hot(childs * quarter, place)
        kids = dot(family, hidden).astype(BF16)
        children[:, b] = kids.reshape(childs, quarter, chans)
        share = spread[:, b].reshape(childs * quarter, chans)
        back = lax.dot_general(family, share, FIRST, preferred_element_type=F32)
        pre_grad[b] = jnp.where(pre > 0, back, 0.0).astype(BF16)
        return carry

    lax.fori_loop(0, live, forward, 0)

    coarse_total = jnp.zeros(coarse.shape, F32)
    for s in range(childs):
        kids = children[s].reshape(blocks * quarter, chans)
        coarse_total += dot(kids, down[s])
        one = lax.dot_general(kids, cgrad[...], FIRST, preferred_element_type=F32)
        part[(kernels + s) * BLOCK : (kernels + s + 1) * BLOCK, :] = one.astype(BF16)
    coarse[...] = coarse_total.astype(BF16)
    used = (kernels + childs) * BLOCK
    if used < part.shape[0]:
        part[used:, :] = jnp.zeros((part.shape[0] - used, part.shape[1]), BF16)

    def backward(k, carry):
        total = jnp.zeros(weight.shape[1:], F32)
        for b in range(0, live, 2):
            group = range(b, min(b + 2, live))
            sums = [dot(pick(k, i), pre_grad[i]).astype(BF16) for i in group]
            sums = jnp.concatenate(sums, axis=0)
            total += dot(jnp.concatenate([table[src[k, i]] for i in group], axis=1), sums)
            terms = lax.dot_general(sums, weight[k], LAST, preferred_element_type=F32)
            for place, i in enumerate(group):
                ext_grad[src[k, i]] += terms[place * BLOCK : (place + 1) * BLOCK]
        part[pl.ds(pl.multiple_of(k * BLOCK, BLOCK), BLOCK), :] = total.astype(BF16)
        return carry

    lax.fori_loop(0, kernels, backward, 0)
    local_grad[...] = ext_grad[:blocks]
    halo_grad[...] = ext_grad[blocks:].reshape(halo_grad.shape).astype(BF16)


def exchange(slab, tile, sems, base):
    me_s, me_t = lax.axis_index("slab"), lax.axis_index("tile")
    steps = ((1, 0), (-1, 0), (0, 1), (0, -1))

    def there(ds, dt):
        s, t = me_s + ds, me_t + dt
        return (s >= 0) & (s < slab) & (t >= 0) & (t < tile)

    def make(d, sign, src, dst):
        ds, dt = steps[d][0] * sign, steps[d][1] * sign
        to = (lax.rem(me_s + ds + slab, slab), lax.rem(me_t + dt + tile, tile))
        send, recv = sems
        return pltpu.make_async_remote_copy(
            src_ref=src, dst_ref=dst, send_sem=send.at[base + d], recv_sem=recv.at[base + d],
            device_id=to, device_id_type=MESH,
        )

    return steps, there, make


def greet_neighbours(slab, tile, barrier):
    me_s, me_t = lax.axis_index("slab"), lax.axis_index("tile")
    steps, there, _ = exchange(slab, tile, None, 0)
    for ds, dt in steps:

        @pl.when(there(ds, dt))
        def _(ds=ds, dt=dt):
            pl.semaphore_signal(
                barrier, inc=1, device_id=(me_s + ds, me_t + dt), device_id_type=MESH
            )


def neighbour_count(slab, tile):
    steps, there, _ = exchange(slab, tile, None, 0)
    return sum(jnp.where(there(ds, dt), 1, 0) for ds, dt in steps)


def send_all(slab, tile, sems, sign, src, dst):
    steps, there, make = exchange(slab, tile, sems, 0)
    for d, (ds, dt) in enumerate(steps):

        @pl.when(there(ds * sign, dt * sign))
        def _(d=d):
            make(d, sign, src.at[d], dst.at[d]).start()


def wait_all(slab, tile, sems, sign, src, dst):
    steps, there, make = exchange(slab, tile, sems, 0)
    for d, (ds, dt) in enumerate(steps):

        @pl.when(there(ds * sign, dt * sign))
        def _(d=d):
            make(d, sign, src.at[d], dst.at[d]).wait_send()

        @pl.when(there(-ds * sign, -dt * sign))
        def _(d=d):
            make(d, sign, src.at[d], dst.at[d]).wait_recv()


def halo_kernel(slab, tile, features, lists, table, outgoing, arrived, send, recv):
    blocks = features.shape[0]
    per_list = outgoing.shape[1]
    arrived[...] = jnp.zeros_like(arrived)
    barrier = pltpu.get_barrier_semaphore()
    greet_neighbours(slab, tile, barrier)
    for n in range(blocks):
        table[n] = features[n].astype(F32).T.astype(BF16)
    local = jnp.concatenate([table[n] for n in range(blocks)], axis=1)
    width = per_list * BLOCK
    for d in range(4):
        rows = hot(blocks * BLOCK, lists[:, d * width : (d + 1) * width])
        picked = dot(local, rows).astype(BF16)
        for j in range(per_list):
            outgoing[d, j] = picked[:, j * BLOCK : (j + 1) * BLOCK]
    pl.semaphore_wait(barrier, neighbour_count(slab, tile))
    send_all(slab, tile, (send, recv), 1, outgoing, arrived)
    wait_all(slab, tile, (send, recv), 1, outgoing, arrived)
    for d in range(4):
        for j in range(per_list):
            table[blocks + d * per_list + j] = arrived[d, j]


def reduce_kernel(
    slab, tile, part, halo, base, lists, total, grad,
    from_pair, after_pair, from_slab, after_slab, from_high, result, coming, send, recv,
):
    high_count = tile // 2
    chunk = part.shape[0] // (slab * tile)
    wide = high_count * chunk
    half = slab * wide
    me_s, me_t = lax.axis_index("slab"), lax.axis_index("tile")
    core, high = lax.rem(me_t, 2), lax.div(me_t, 2)
    pair = me_t + 1 - 2 * core

    def rows(start, count):
        return pl.ds(pl.multiple_of(start, 16), count)

    def remote(src, dst, i, s, t):
        return pltpu.make_async_remote_copy(
            src_ref=src, dst_ref=dst, send_sem=send.at[i], recv_sem=recv.at[i],
            device_id=(s, t), device_id_type=MESH,
        )

    slab_peers = [lax.rem(me_s + d, slab) for d in range(1, slab)]
    high_peers = [lax.rem(high + d, high_count) for d in range(1, high_count)]

    coming[...] = jnp.zeros_like(coming)
    barrier = pltpu.get_barrier_semaphore()
    greeted = [(me_s, pair)] + [(s, me_t) for s in slab_peers] + [(me_s, h * 2 + core) for h in high_peers]
    for to in greeted:
        pl.semaphore_signal(barrier, inc=1, device_id=to, device_id_type=MESH)
    beside = me_t + 2 * core - 1
    has_beside = (beside >= 0) & (beside < tile)

    @pl.when(has_beside)
    def _():
        pl.semaphore_signal(barrier, inc=1, device_id=(me_s, beside), device_id_type=MESH)

    pl.semaphore_wait(barrier, len(greeted) + jnp.where(has_beside, 1, 0))

    first = remote(part.at[rows((1 - core) * half, half)], from_pair, 4, me_s, pair)
    first.start()
    send_all(slab, tile, (send, recv), -1, halo, coming)
    first.wait()
    mine = part[rows(core * half, half), :].astype(F32) + from_pair[...].astype(F32)
    after_pair[...] = mine.astype(BF16)

    at = 5
    copies = []
    for d, s in enumerate(slab_peers):
        src = after_pair.at[rows(s * wide, wide)]
        copies.append(remote(src, from_slab.at[d], at + d, s, me_t))
        copies[-1].start()
    at += len(slab_peers)

    wait_all(slab, tile, (send, recv), -1, halo, coming)
    blocks = grad.shape[0]
    back = coming[...].reshape(-1, coming.shape[-1])
    for n in range(blocks):
        grad[n] = base[n] + dot(hot(BLOCK, lists[...] - n * BLOCK), back)

    for copy in copies:
        copy.wait()
    mine = after_pair[rows(me_s * wide, wide), :].astype(F32)
    for d in range(len(slab_peers)):
        mine += from_slab[d].astype(F32)
    after_slab[...] = mine.astype(BF16)

    copies = []
    for d, h in enumerate(high_peers):
        src = after_slab.at[rows(h * chunk, chunk)]
        copies.append(remote(src, from_high.at[d], at + d, me_s, h * 2 + core))
        copies[-1].start()
    at += len(high_peers)
    for copy in copies:
        copy.wait()
    mine = after_slab[rows(high * chunk, chunk), :].astype(F32)
    for d in range(len(high_peers)):
        mine += from_high[d].astype(F32)
    own = rows(((core * slab + me_s) * high_count + high) * chunk, chunk)
    result[own, :] = mine.astype(BF16)

    def share(where, peers, at):
        copies = [remote(result.at[where], result.at[where], at + d, s, t) for d, (s, t) in enumerate(peers)]
        for copy in copies:
            copy.start()
        for copy in copies:
            copy.wait()
        return at + len(peers)

    at = share(own, [(me_s, h * 2 + core) for h in high_peers], at)
    at = share(rows((core * slab + me_s) * wide, wide), [(s, me_t) for s in slab_peers], at)
    share(rows(core * half, half), [(me_s, pair)], at)
    total[...] = result[...]


def body(features, conv_weight, down_weight, coarse_grad, rulebook, boundary_rows, parent_code):
    rows, chans = features.shape
    coarse_rows, out_chans = coarse_grad.shape
    list_len = boundary_rows.shape[1]
    childs = down_weight.shape[0]
    kernels = conv_weight.shape[0]
    blocks = rows // BLOCK
    per_list = list_len // BLOCK
    total_blocks = blocks + 4 * per_list
    slab, tile = lax.axis_size("slab"), lax.axis_size("tile")
    high_count = tile // 2
    used = (kernels + childs) * BLOCK
    chunk = -(-used // (16 * slab * tile)) * 16
    vmem = pl.BlockSpec(memory_space=pltpu.VMEM)
    lists = boundary_rows.reshape(1, 4 * list_len)

    table = pl.pallas_call(
        functools.partial(halo_kernel, slab, tile),
        out_shape=jax.ShapeDtypeStruct((total_blocks, chans, BLOCK), BF16),
        in_specs=[vmem] * 2,
        out_specs=vmem,
        scratch_shapes=[
            pltpu.VMEM((4, per_list, chans, BLOCK), BF16),
            pltpu.VMEM((4, per_list, chans, BLOCK), BF16),
            pltpu.SemaphoreType.DMA((4,)),
            pltpu.SemaphoreType.DMA((4,)),
        ],
        compiler_params=pltpu.CompilerParams(
            collective_id=0, has_side_effects=True, vmem_limit_bytes=32 * 2**20
        ),
        name="halo",
    )(features.reshape(blocks, BLOCK, chans), lists)
    wflat = conv_weight.transpose(2, 0, 1).reshape(out_chans, kernels * chans)
    book = rulebook.reshape(kernels, blocks, BLOCK)
    src = jnp.minimum(jnp.min(book, axis=2) // BLOCK, total_blocks - 1)
    coarse, part, local_grad, halo_grad = pl.pallas_call(
        main_kernel,
        out_shape=(
            jax.ShapeDtypeStruct((coarse_rows, out_chans), BF16),
            jax.ShapeDtypeStruct((chunk * slab * tile, out_chans), BF16),
            jax.ShapeDtypeStruct((blocks, BLOCK, chans), F32),
            jax.ShapeDtypeStruct((4, list_len, chans), BF16),
        ),
        in_specs=[pl.BlockSpec(memory_space=pltpu.SMEM)] + [vmem] * 7,
        out_specs=(vmem,) * 4,
        scratch_shapes=[
            pltpu.VMEM((total_blocks, BLOCK, chans), F32),
            pltpu.VMEM((kernels * BLOCK, BLOCK), BF16),
            pltpu.VMEM((blocks, BLOCK, chans), BF16),
            pltpu.VMEM((childs, blocks, coarse_rows // blocks, chans), BF16),
            pltpu.VMEM((childs, blocks, coarse_rows // blocks, chans), BF16),
        ],
        compiler_params=pltpu.CompilerParams(vmem_limit_bytes=40 * 2**20),
        name="sparse_conv",
    )(
        src, table, wflat, conv_weight, down_weight, coarse_grad, book,
        parent_code.reshape(blocks, BLOCK),
    )
    wide = high_count * chunk
    copies = 4 + 2 * (1 + (slab - 1) + (high_count - 1))
    total, input_grad = pl.pallas_call(
        functools.partial(reduce_kernel, slab, tile),
        out_shape=(
            jax.ShapeDtypeStruct(part.shape, BF16),
            jax.ShapeDtypeStruct((blocks, BLOCK, chans), F32),
        ),
        in_specs=[vmem] * 4,
        out_specs=(vmem,) * 2,
        scratch_shapes=[
            pltpu.VMEM((slab * wide, out_chans), BF16),
            pltpu.VMEM((slab * wide, out_chans), BF16),
            pltpu.VMEM((slab - 1, wide, out_chans), BF16),
            pltpu.VMEM((wide, out_chans), BF16),
            pltpu.VMEM((high_count - 1, chunk, out_chans), BF16),
            pltpu.VMEM(part.shape, BF16),
            pltpu.VMEM((4, list_len, chans), BF16),
            pltpu.SemaphoreType.DMA((copies,)),
            pltpu.SemaphoreType.DMA((copies,)),
        ],
        compiler_params=pltpu.CompilerParams(
            collective_id=1, has_side_effects=True, vmem_limit_bytes=32 * 2**20
        ),
        name="reduce",
    )(part, halo_grad, local_grad, lists)
    total = total.astype(F32)
    conv_grad = total[: kernels * BLOCK].reshape(conv_weight.shape)
    down_grad = total[kernels * BLOCK : used].reshape(down_weight.shape)
    return (coarse, input_grad.reshape(rows, chans), conv_grad, down_grad)


def solution(mesh):
    return jax.shard_map(
        body,
        mesh=mesh,
        in_specs=(
            P(("slab", "tile"), None),
            P(),
            P(),
            P(("slab", "tile"), None),
            P(None, ("slab", "tile")),
            P(("slab", "tile"), None),
            P(("slab", "tile")),
        ),
        out_specs=(P(("slab", "tile"), None), P(("slab", "tile"), None), P(), P()),
        check_vma=False,
    )
```

```python
import functools

import jax
import jax.numpy as jnp
from jax import lax
from jax.experimental import pallas as pl
from jax.experimental.pallas import tpu as pltpu
from jax.sharding import PartitionSpec as P

BLOCK = 128
GROUP = 3
F32 = jnp.float32
BF16 = jnp.bfloat16
LAST = (((1,), (1,)), ((), ()))
FIRST = (((0,), (0,)), ((), ()))
MESH = pl.DeviceIdType.MESH


def dot(a, b):
    return jnp.dot(a, b, preferred_element_type=F32)


def hot(rows, index):
    short = jnp.clip(index, -1, rows).astype(jnp.int16)
    same = lax.broadcasted_iota(jnp.int16, (rows, index.shape[1]), 0) == short
    return jnp.where(same, jnp.ones((), BF16), jnp.zeros((), BF16))


def diagonal(first, second):
    empty = jnp.zeros_like(first)
    top = jnp.concatenate([first, empty], axis=1)
    return jnp.concatenate([top, jnp.concatenate([empty, second], axis=1)], axis=0)


def main_kernel(
    src, table, wflat, weight, down, cgrad, book, code,
    coarse, part, local_grad, halo_grad,
    ext_grad, gathered, pre_grad, sums, spread, children,
):
    kernels, blocks = book.shape[0], book.shape[1]
    childs, _, quarter, chans = spread.shape
    pairs = blocks // 2
    group = sums.shape[0]
    ext_grad[...] = jnp.zeros_like(ext_grad)
    children[...] = jnp.zeros_like(children)
    for s in range(childs):
        one = lax.dot_general(cgrad[...], down[s], LAST, preferred_element_type=F32)
        spread[s] = one.astype(BF16).reshape(blocks, quarter, chans)

    def pick(k, b):
        return hot(BLOCK, book[k, pl.ds(b, 1), :] - src[k, b] * BLOCK)

    def pair_of(k, p):
        return jnp.concatenate([table[src[k, 2 * p]], table[src[k, 2 * p + 1]]], axis=1)

    def forward(p, carry):
        for k in range(kernels):
            got = dot(pair_of(k, p), diagonal(pick(k, 2 * p), pick(k, 2 * p + 1)))
            gathered[k * BLOCK : (k + 1) * BLOCK, :] = got.astype(BF16)
        pre_both = dot(wflat[...], gathered[...])
        grads = []
        for i in range(2):
            b = 2 * p + i
            pre = pre_both[:, i * BLOCK : (i + 1) * BLOCK].T
            hidden = jnp.maximum(pre, 0.0).astype(BF16)
            own = code[pl.ds(b, 1), :]
            place = (own % childs) * quarter + (own // childs - b * quarter)
            place = jnp.where(own // childs < blocks * quarter, place, -1)
            family = hot(childs * quarter, place)
            kids = dot(family, hidden).astype(BF16)
            children[:, b] = kids.reshape(childs, quarter, chans)
            share = spread[:, b].reshape(childs * quarter, chans)
            back = lax.dot_general(family, share, FIRST, preferred_element_type=F32)
            grads.append(jnp.where(pre > 0, back, 0.0).astype(BF16))
        pre_grad[p] = diagonal(*grads)
        return carry

    lax.fori_loop(0, pairs, forward, 0)

    coarse_total = jnp.zeros(coarse.shape, F32)
    for s in range(childs):
        kids = children[s].reshape(blocks * quarter, chans)
        coarse_total += dot(kids, down[s])
        one = lax.dot_general(kids, cgrad[...], FIRST, preferred_element_type=F32)
        part[(kernels + s) * BLOCK : (kernels + s + 1) * BLOCK, :] = one.astype(BF16)
    coarse[...] = coarse_total.astype(BF16)
    used = (kernels + childs) * BLOCK
    if used < part.shape[0]:
        part[used:, :] = jnp.zeros((part.shape[0] - used, part.shape[1]), BF16)

    def backward(step, carry):
        first = step * group
        for p in range(pairs):
            picks = [
                jnp.concatenate([pick(first + g, 2 * p), pick(first + g, 2 * p + 1)], axis=1)
                for g in range(group)
            ]
            both = dot(jnp.concatenate(picks, axis=0), pre_grad[p]).astype(BF16)
            for g in range(group):
                sums[g, p] = both[g * BLOCK : (g + 1) * BLOCK]
        for g in range(group):
            k = first + g
            twice = diagonal(weight[k], weight[k])
            total = jnp.zeros(weight.shape[1:], F32)
            for p in range(pairs):
                both = sums[g, p]
                terms = lax.dot_general(both, twice, LAST, preferred_element_type=F32)
                stacked = jnp.concatenate([both[:, :BLOCK], both[:, BLOCK:]], axis=0)
                total += dot(pair_of(k, p), stacked)
                for i in range(2):
                    ext_grad[src[k, 2 * p + i]] += terms[:, i * BLOCK : (i + 1) * BLOCK]
            part[pl.ds(pl.multiple_of(k * BLOCK, BLOCK), BLOCK), :] = total.astype(BF16)
        return carry

    lax.fori_loop(0, kernels // group, backward, 0)
    local_grad[...] = ext_grad[:blocks]
    halo_grad[...] = ext_grad[blocks:].reshape(halo_grad.shape).astype(BF16)


def exchange(slab, tile, sems, base):
    me_s, me_t = lax.axis_index("slab"), lax.axis_index("tile")
    steps = ((1, 0), (-1, 0), (0, 1), (0, -1))

    def there(ds, dt):
        s, t = me_s + ds, me_t + dt
        return (s >= 0) & (s < slab) & (t >= 0) & (t < tile)

    def make(d, sign, src, dst):
        ds, dt = steps[d][0] * sign, steps[d][1] * sign
        to = (lax.rem(me_s + ds + slab, slab), lax.rem(me_t + dt + tile, tile))
        send, recv = sems
        return pltpu.make_async_remote_copy(
            src_ref=src, dst_ref=dst, send_sem=send.at[base + d], recv_sem=recv.at[base + d],
            device_id=to, device_id_type=MESH,
        )

    return steps, there, make


def greet_neighbours(slab, tile, barrier):
    me_s, me_t = lax.axis_index("slab"), lax.axis_index("tile")
    steps, there, _ = exchange(slab, tile, None, 0)
    for ds, dt in steps:

        @pl.when(there(ds, dt))
        def _(ds=ds, dt=dt):
            pl.semaphore_signal(
                barrier, inc=1, device_id=(me_s + ds, me_t + dt), device_id_type=MESH
            )


def neighbour_count(slab, tile):
    steps, there, _ = exchange(slab, tile, None, 0)
    return sum(jnp.where(there(ds, dt), 1, 0) for ds, dt in steps)


def send_all(slab, tile, sems, sign, src, dst):
    steps, there, make = exchange(slab, tile, sems, 0)
    for d, (ds, dt) in enumerate(steps):

        @pl.when(there(ds * sign, dt * sign))
        def _(d=d):
            make(d, sign, src.at[d], dst.at[d]).start()


def wait_all(slab, tile, sems, sign, src, dst):
    steps, there, make = exchange(slab, tile, sems, 0)
    for d, (ds, dt) in enumerate(steps):

        @pl.when(there(ds * sign, dt * sign))
        def _(d=d):
            make(d, sign, src.at[d], dst.at[d]).wait_send()

        @pl.when(there(-ds * sign, -dt * sign))
        def _(d=d):
            make(d, sign, src.at[d], dst.at[d]).wait_recv()


def halo_kernel(slab, tile, features, lists, table, outgoing, arrived, send, recv):
    blocks = features.shape[0]
    per_list = outgoing.shape[1]
    arrived[...] = jnp.zeros_like(arrived)
    barrier = pltpu.get_barrier_semaphore()
    greet_neighbours(slab, tile, barrier)
    for n in range(blocks):
        table[n] = features[n].astype(F32).T.astype(BF16)
    local = jnp.concatenate([table[n] for n in range(blocks)], axis=1)
    width = per_list * BLOCK
    for d in range(4):
        rows = hot(blocks * BLOCK, lists[:, d * width : (d + 1) * width])
        picked = dot(local, rows).astype(BF16)
        for j in range(per_list):
            outgoing[d, j] = picked[:, j * BLOCK : (j + 1) * BLOCK]
    pl.semaphore_wait(barrier, neighbour_count(slab, tile))
    send_all(slab, tile, (send, recv), 1, outgoing, arrived)
    wait_all(slab, tile, (send, recv), 1, outgoing, arrived)
    for d in range(4):
        for j in range(per_list):
            table[blocks + d * per_list + j] = arrived[d, j]


def reduce_kernel(
    slab, tile, part, halo, base, lists, total, grad,
    from_pair, after_pair, from_slab, after_slab, from_high, result, coming, send, recv,
):
    high_count = tile // 2
    chunk = part.shape[0] // (slab * tile)
    wide = high_count * chunk
    half = slab * wide
    me_s, me_t = lax.axis_index("slab"), lax.axis_index("tile")
    core, high = lax.rem(me_t, 2), lax.div(me_t, 2)
    pair = me_t + 1 - 2 * core

    def rows(start, count):
        return pl.ds(pl.multiple_of(start, 16), count)

    def remote(src, dst, i, s, t):
        return pltpu.make_async_remote_copy(
            src_ref=src, dst_ref=dst, send_sem=send.at[i], recv_sem=recv.at[i],
            device_id=(s, t), device_id_type=MESH,
        )

    slab_peers = [lax.rem(me_s + d, slab) for d in range(1, slab)]
    high_peers = [lax.rem(high + d, high_count) for d in range(1, high_count)]

    coming[...] = jnp.zeros_like(coming)
    barrier = pltpu.get_barrier_semaphore()
    greeted = [(me_s, pair)] + [(s, me_t) for s in slab_peers] + [(me_s, h * 2 + core) for h in high_peers]
    for to in greeted:
        pl.semaphore_signal(barrier, inc=1, device_id=to, device_id_type=MESH)
    beside = me_t + 2 * core - 1
    has_beside = (beside >= 0) & (beside < tile)

    @pl.when(has_beside)
    def _():
        pl.semaphore_signal(barrier, inc=1, device_id=(me_s, beside), device_id_type=MESH)

    pl.semaphore_wait(barrier, len(greeted) + jnp.where(has_beside, 1, 0))

    first = remote(part.at[rows((1 - core) * half, half)], from_pair, 4, me_s, pair)
    first.start()
    send_all(slab, tile, (send, recv), -1, halo, coming)
    first.wait()
    mine = part[rows(core * half, half), :].astype(F32) + from_pair[...].astype(F32)
    after_pair[...] = mine.astype(BF16)

    at = 5
    copies = []
    for d, s in enumerate(slab_peers):
        src = after_pair.at[rows(s * wide, wide)]
        copies.append(remote(src, from_slab.at[d], at + d, s, me_t))
        copies[-1].start()
    at += len(slab_peers)

    wait_all(slab, tile, (send, recv), -1, halo, coming)
    blocks = grad.shape[0]
    back = coming[...].reshape(-1, coming.shape[-1])
    for n in range(blocks):
        grad[n] = base[n] + dot(hot(BLOCK, lists[...] - n * BLOCK), back)

    for copy in copies:
        copy.wait()
    mine = after_pair[rows(me_s * wide, wide), :].astype(F32)
    for d in range(len(slab_peers)):
        mine += from_slab[d].astype(F32)
    after_slab[...] = mine.astype(BF16)

    copies = []
    for d, h in enumerate(high_peers):
        src = after_slab.at[rows(h * chunk, chunk)]
        copies.append(remote(src, from_high.at[d], at + d, me_s, h * 2 + core))
        copies[-1].start()
    at += len(high_peers)
    for copy in copies:
        copy.wait()
    mine = after_slab[rows(high * chunk, chunk), :].astype(F32)
    for d in range(len(high_peers)):
        mine += from_high[d].astype(F32)
    own = rows(((core * slab + me_s) * high_count + high) * chunk, chunk)
    result[own, :] = mine.astype(BF16)

    def share(where, peers, at):
        copies = [remote(result.at[where], result.at[where], at + d, s, t) for d, (s, t) in enumerate(peers)]
        for copy in copies:
            copy.start()
        for copy in copies:
            copy.wait()
        return at + len(peers)

    at = share(own, [(me_s, h * 2 + core) for h in high_peers], at)
    at = share(rows((core * slab + me_s) * wide, wide), [(s, me_t) for s in slab_peers], at)
    share(rows(core * half, half), [(me_s, pair)], at)
    total[...] = result[...]


def body(features, conv_weight, down_weight, coarse_grad, rulebook, boundary_rows, parent_code):
    rows, chans = features.shape
    coarse_rows, out_chans = coarse_grad.shape
    list_len = boundary_rows.shape[1]
    childs = down_weight.shape[0]
    kernels = conv_weight.shape[0]
    blocks = rows // BLOCK
    per_list = list_len // BLOCK
    total_blocks = blocks + 4 * per_list
    slab, tile = lax.axis_size("slab"), lax.axis_size("tile")
    high_count = tile // 2
    used = (kernels + childs) * BLOCK
    chunk = -(-used // (16 * slab * tile)) * 16
    vmem = pl.BlockSpec(memory_space=pltpu.VMEM)
    lists = boundary_rows.reshape(1, 4 * list_len)

    table = pl.pallas_call(
        functools.partial(halo_kernel, slab, tile),
        out_shape=jax.ShapeDtypeStruct((total_blocks, chans, BLOCK), BF16),
        in_specs=[vmem] * 2,
        out_specs=vmem,
        scratch_shapes=[
            pltpu.VMEM((4, per_list, chans, BLOCK), BF16),
            pltpu.VMEM((4, per_list, chans, BLOCK), BF16),
            pltpu.SemaphoreType.DMA((4,)),
            pltpu.SemaphoreType.DMA((4,)),
        ],
        compiler_params=pltpu.CompilerParams(
            collective_id=0, has_side_effects=True, vmem_limit_bytes=32 * 2**20
        ),
        name="halo",
    )(features.reshape(blocks, BLOCK, chans), lists)
    wflat = conv_weight.transpose(2, 0, 1).reshape(out_chans, kernels * chans)
    book = rulebook.reshape(kernels, blocks, BLOCK)
    src = jnp.minimum(jnp.min(book, axis=2) // BLOCK, total_blocks - 1)
    coarse, part, local_grad, halo_grad = pl.pallas_call(
        main_kernel,
        out_shape=(
            jax.ShapeDtypeStruct((coarse_rows, out_chans), BF16),
            jax.ShapeDtypeStruct((chunk * slab * tile, out_chans), BF16),
            jax.ShapeDtypeStruct((blocks, BLOCK, chans), F32),
            jax.ShapeDtypeStruct((4, list_len, chans), BF16),
        ),
        in_specs=[pl.BlockSpec(memory_space=pltpu.SMEM)] + [vmem] * 7,
        out_specs=(vmem,) * 4,
        scratch_shapes=[
            pltpu.VMEM((total_blocks, BLOCK, chans), F32),
            pltpu.VMEM((kernels * BLOCK, 2 * BLOCK), BF16),
            pltpu.VMEM((blocks // 2, 2 * BLOCK, 2 * chans), BF16),
            pltpu.VMEM((GROUP, blocks // 2, BLOCK, 2 * chans), BF16),
            pltpu.VMEM((childs, blocks, coarse_rows // blocks, chans), BF16),
            pltpu.VMEM((childs, blocks, coarse_rows // blocks, chans), BF16),
        ],
        compiler_params=pltpu.CompilerParams(vmem_limit_bytes=40 * 2**20),
        name="sparse_conv",
    )(
        src, table, wflat, conv_weight, down_weight, coarse_grad, book,
        parent_code.reshape(blocks, BLOCK),
    )
    wide = high_count * chunk
    copies = 4 + 2 * (1 + (slab - 1) + (high_count - 1))
    total, input_grad = pl.pallas_call(
        functools.partial(reduce_kernel, slab, tile),
        out_shape=(
            jax.ShapeDtypeStruct(part.shape, BF16),
            jax.ShapeDtypeStruct((blocks, BLOCK, chans), F32),
        ),
        in_specs=[vmem] * 4,
        out_specs=(vmem,) * 2,
        scratch_shapes=[
            pltpu.VMEM((slab * wide, out_chans), BF16),
            pltpu.VMEM((slab * wide, out_chans), BF16),
            pltpu.VMEM((slab - 1, wide, out_chans), BF16),
            pltpu.VMEM((wide, out_chans), BF16),
            pltpu.VMEM((high_count - 1, chunk, out_chans), BF16),
            pltpu.VMEM(part.shape, BF16),
            pltpu.VMEM((4, list_len, chans), BF16),
            pltpu.SemaphoreType.DMA((copies,)),
            pltpu.SemaphoreType.DMA((copies,)),
        ],
        compiler_params=pltpu.CompilerParams(
            collective_id=1, has_side_effects=True, vmem_limit_bytes=32 * 2**20
        ),
        name="reduce",
    )(part, halo_grad, local_grad, lists)
    total = total.astype(F32)
    conv_grad = total[: kernels * BLOCK].reshape(conv_weight.shape)
    down_grad = total[kernels * BLOCK : used].reshape(down_weight.shape)
    return (coarse, input_grad.reshape(rows, chans), conv_grad, down_grad)


def solution(mesh):
    return jax.shard_map(
        body,
        mesh=mesh,
        in_specs=(
            P(("slab", "tile"), None),
            P(),
            P(),
            P(("slab", "tile"), None),
            P(None, ("slab", "tile")),
            P(("slab", "tile"), None),
            P(("slab", "tile")),
        ),
        out_specs=(P(("slab", "tile"), None), P(("slab", "tile"), None), P(), P()),
        check_vma=False,
    )
```

```python
import functools

import jax
import jax.numpy as jnp
from jax import lax
from jax.experimental import pallas as pl
from jax.experimental.pallas import tpu as pltpu
from jax.sharding import PartitionSpec as P

BLOCK = 128
GROUP = 3
F32 = jnp.float32
BF16 = jnp.bfloat16
LAST = (((1,), (1,)), ((), ()))
FIRST = (((0,), (0,)), ((), ()))
MESH = pl.DeviceIdType.MESH


def dot(a, b):
    return jnp.dot(a, b, preferred_element_type=F32)


def hot(rows, index):
    short = jnp.clip(index, -1, rows).astype(jnp.int16)
    same = lax.broadcasted_iota(jnp.int16, (rows, index.shape[1]), 0) == short
    return jnp.where(same, jnp.ones((), BF16), jnp.zeros((), BF16))


def diagonal(first, second):
    empty = jnp.zeros_like(first)
    top = jnp.concatenate([first, empty], axis=1)
    return jnp.concatenate([top, jnp.concatenate([empty, second], axis=1)], axis=0)


def main_kernel(
    src, table, wflat, weight, down, cgrad, book, code,
    coarse, part, local_grad, halo_grad,
    ext_grad, gathered, pre_grad, sums, spread, children,
):
    kernels, blocks = book.shape[0], book.shape[1]
    childs, _, quarter, chans = spread.shape
    pairs = blocks // 2
    group = sums.shape[0]
    ext_grad[...] = jnp.zeros_like(ext_grad)
    children[...] = jnp.zeros_like(children)
    for s in range(childs):
        one = lax.dot_general(cgrad[...], down[s], LAST, preferred_element_type=F32)
        spread[s] = one.astype(BF16).reshape(blocks, quarter, chans)

    def pick(k, b):
        return hot(BLOCK, book[k, pl.ds(b, 1), :] - src[k, b] * BLOCK)

    def pair_of(k, p):
        return jnp.concatenate([table[src[k, 2 * p]], table[src[k, 2 * p + 1]]], axis=1)

    def forward(p, carry):
        for k in range(kernels):
            got = dot(pair_of(k, p), diagonal(pick(k, 2 * p), pick(k, 2 * p + 1)))
            gathered[k * BLOCK : (k + 1) * BLOCK, :] = got.astype(BF16)
        pre_both = dot(wflat[...], gathered[...])
        grads = []
        for i in range(2):
            b = 2 * p + i
            pre = pre_both[:, i * BLOCK : (i + 1) * BLOCK].T
            hidden = jnp.maximum(pre, 0.0).astype(BF16)
            own = code[pl.ds(b, 1), :]
            place = (own % childs) * quarter + (own // childs - b * quarter)
            place = jnp.where(own // childs < blocks * quarter, place, -1)
            family = hot(childs * quarter, place)
            kids = dot(family, hidden).astype(BF16)
            children[:, b] = kids.reshape(childs, quarter, chans)
            share = spread[:, b].reshape(childs * quarter, chans)
            back = lax.dot_general(family, share, FIRST, preferred_element_type=F32)
            grads.append(jnp.where(pre > 0, back, 0.0).astype(BF16))
        pre_grad[p] = diagonal(*grads)
        return carry

    lax.fori_loop(0, pairs, forward, 0)

    coarse_total = jnp.zeros(coarse.shape, F32)
    for s in range(childs):
        kids = children[s].reshape(blocks * quarter, chans)
        coarse_total += dot(kids, down[s])
        one = lax.dot_general(kids, cgrad[...], FIRST, preferred_element_type=F32)
        part[(kernels + s) * BLOCK : (kernels + s + 1) * BLOCK, :] = one.astype(BF16)
    coarse[...] = coarse_total.astype(BF16)
    used = (kernels + childs) * BLOCK
    if used < part.shape[0]:
        part[used:, :] = jnp.zeros((part.shape[0] - used, part.shape[1]), BF16)

    def backward(step, carry):
        first = step * group
        for p in range(pairs):
            picks = [
                jnp.concatenate([pick(first + g, 2 * p), pick(first + g, 2 * p + 1)], axis=1)
                for g in range(group)
            ]
            both = dot(jnp.concatenate(picks, axis=0), pre_grad[p]).astype(BF16)
            for g in range(group):
                sums[g, p] = both[g * BLOCK : (g + 1) * BLOCK]
        for g in range(group):
            k = first + g
            twice = diagonal(weight[k], weight[k])
            total = jnp.zeros(weight.shape[1:], F32)
            for p in range(pairs):
                both = sums[g, p]
                terms = lax.dot_general(both, twice, LAST, preferred_element_type=F32)
                stacked = jnp.concatenate([both[:, :BLOCK], both[:, BLOCK:]], axis=0)
                total += dot(pair_of(k, p), stacked)
                for i in range(2):
                    ext_grad[src[k, 2 * p + i]] += terms[:, i * BLOCK : (i + 1) * BLOCK]
            part[pl.ds(pl.multiple_of(k * BLOCK, BLOCK), BLOCK), :] = total.astype(BF16)
        return carry

    lax.fori_loop(0, kernels // group, backward, 0)
    local_grad[...] = ext_grad[:blocks]
    halo_grad[...] = ext_grad[blocks:].reshape(halo_grad.shape).astype(BF16)


def exchange(slab, tile, sems, base):
    me_s, me_t = lax.axis_index("slab"), lax.axis_index("tile")
    steps = ((1, 0), (-1, 0), (0, 1), (0, -1))

    def there(ds, dt):
        s, t = me_s + ds, me_t + dt
        return (s >= 0) & (s < slab) & (t >= 0) & (t < tile)

    def make(d, sign, src, dst):
        ds, dt = steps[d][0] * sign, steps[d][1] * sign
        to = (lax.rem(me_s + ds + slab, slab), lax.rem(me_t + dt + tile, tile))
        send, recv = sems
        return pltpu.make_async_remote_copy(
            src_ref=src, dst_ref=dst, send_sem=send.at[base + d], recv_sem=recv.at[base + d],
            device_id=to, device_id_type=MESH,
        )

    return steps, there, make


def greet_neighbours(slab, tile, barrier):
    me_s, me_t = lax.axis_index("slab"), lax.axis_index("tile")
    steps, there, _ = exchange(slab, tile, None, 0)
    for ds, dt in steps:

        @pl.when(there(ds, dt))
        def _(ds=ds, dt=dt):
            pl.semaphore_signal(
                barrier, inc=1, device_id=(me_s + ds, me_t + dt), device_id_type=MESH
            )


def neighbour_count(slab, tile):
    steps, there, _ = exchange(slab, tile, None, 0)
    return sum(jnp.where(there(ds, dt), 1, 0) for ds, dt in steps)


def send_all(slab, tile, sems, sign, src, dst):
    steps, there, make = exchange(slab, tile, sems, 0)
    for d, (ds, dt) in enumerate(steps):

        @pl.when(there(ds * sign, dt * sign))
        def _(d=d):
            make(d, sign, src.at[d], dst.at[d]).start()


def wait_all(slab, tile, sems, sign, src, dst):
    steps, there, make = exchange(slab, tile, sems, 0)
    for d, (ds, dt) in enumerate(steps):

        @pl.when(there(ds * sign, dt * sign))
        def _(d=d):
            make(d, sign, src.at[d], dst.at[d]).wait_send()

        @pl.when(there(-ds * sign, -dt * sign))
        def _(d=d):
            make(d, sign, src.at[d], dst.at[d]).wait_recv()


def halo_kernel(slab, tile, features, lists, table, outgoing, arrived, send, recv):
    blocks = features.shape[0]
    per_list = outgoing.shape[1]
    arrived[...] = jnp.zeros_like(arrived)
    barrier = pltpu.get_barrier_semaphore()
    greet_neighbours(slab, tile, barrier)
    for n in range(blocks):
        table[n] = features[n].astype(F32).T.astype(BF16)
    local = jnp.concatenate([table[n] for n in range(blocks)], axis=1)
    width = per_list * BLOCK
    for d in range(4):
        rows = hot(blocks * BLOCK, lists[:, d * width : (d + 1) * width])
        picked = dot(local, rows).astype(BF16)
        for j in range(per_list):
            outgoing[d, j] = picked[:, j * BLOCK : (j + 1) * BLOCK]
    pl.semaphore_wait(barrier, neighbour_count(slab, tile))
    send_all(slab, tile, (send, recv), 1, outgoing, arrived)
    wait_all(slab, tile, (send, recv), 1, outgoing, arrived)
    for d in range(4):
        for j in range(per_list):
            table[blocks + d * per_list + j] = arrived[d, j]


def reduce_kernel(slab, tile, pieces, part, halo, base, lists, total, grad, result, coming, send, recv, *buffers):
    high_count = tile // 2
    me_s, me_t = lax.axis_index("slab"), lax.axis_index("tile")
    core, high = lax.rem(me_t, 2), lax.div(me_t, 2)
    pair = me_t + 1 - 2 * core

    def rows(start, count):
        return pl.ds(pl.multiple_of(start, 16), count)

    def remote(src, dst, i, to):
        return pltpu.make_async_remote_copy(
            src_ref=src, dst_ref=dst, send_sem=send.at[i], recv_sem=recv.at[i],
            device_id=to, device_id_type=MESH,
        )

    slab_peers = [lax.rem(me_s + d, slab) for d in range(1, slab)]
    high_peers = [lax.rem(high + d, high_count) for d in range(1, high_count)]
    along_slab = (slab, me_s, [(s, (s, me_t)) for s in slab_peers])
    along_high = (high_count, high, [(h, (me_s, h * 2 + core)) for h in high_peers])
    one_way = 1 + len(slab_peers) + len(high_peers)

    def flow(start, piece, outer, inner, at, from_pair, after_pair, from_outer, after_outer, from_inner):
        outer_count, outer_me, outer_peers = outer
        inner_count, inner_me, inner_peers = inner
        wide = inner_count * piece
        half = outer_count * wide

        def scatter(held, size, landing, peers, at):
            copies = []
            for d, (index, to) in enumerate(peers):
                copies.append(remote(held.at[rows(index * size, size)], landing.at[d], at + d, to))
                copies[-1].start()
            return copies

        def share(first_row, count, devices, at):
            where = rows(first_row, count)
            copies = [remote(result.at[where], result.at[where], at + d, to) for d, to in enumerate(devices)]
            for copy in copies:
                copy.start()
            return copies

        def wait(copies):
            for copy in copies:
                copy.wait()

        def summed(held, size, me, landing, peers):
            mine = held[rows(me * size, size), :].astype(F32)
            for d in range(len(peers)):
                mine += landing[d].astype(F32)
            return mine.astype(BF16)

        first = remote(part.at[rows(start + (1 - core) * half, half)], from_pair, at, (me_s, pair))
        first.start()
        yield
        first.wait()
        mine = part[rows(start + core * half, half), :].astype(F32) + from_pair[...].astype(F32)
        after_pair[...] = mine.astype(BF16)
        copies = scatter(after_pair, wide, from_outer, outer_peers, at + 1)
        yield
        wait(copies)
        after_outer[...] = summed(after_pair, wide, outer_me, from_outer, outer_peers)
        copies = scatter(after_outer, piece, from_inner, inner_peers, at + 1 + len(outer_peers))
        yield
        wait(copies)
        own_half = start + core * half
        own_wide = own_half + outer_me * wide
        own = own_wide + inner_me * piece
        result[rows(own, piece), :] = summed(after_outer, piece, inner_me, from_inner, inner_peers)
        at += one_way
        copies = share(own, piece, [to for _, to in inner_peers], at)
        yield
        wait(copies)
        copies = share(own_wide, wide, [to for _, to in outer_peers], at + len(inner_peers))
        yield
        wait(copies)
        copies = share(own_half, half, [(me_s, pair)], at + one_way - 1)
        yield
        wait(copies)
        yield

    coming[...] = jnp.zeros_like(coming)
    barrier = pltpu.get_barrier_semaphore()
    greeted = [(me_s, pair)] + [to for _, to in along_slab[2]] + [to for _, to in along_high[2]]
    for to in greeted:
        pl.semaphore_signal(barrier, inc=1, device_id=to, device_id_type=MESH)
    beside = me_t + 2 * core - 1
    has_beside = (beside >= 0) & (beside < tile)

    @pl.when(has_beside)
    def _():
        pl.semaphore_signal(barrier, inc=1, device_id=(me_s, beside), device_id_type=MESH)

    pl.semaphore_wait(barrier, len(greeted) + jnp.where(has_beside, 1, 0))

    count = len(buffers) // 2
    flows = [
        flow(0, pieces[0], along_slab, along_high, 4, *buffers[:count]),
        flow(pieces[0] * slab * tile, pieces[1], along_high, along_slab, 4 + 2 * one_way, *buffers[count:]),
    ]
    for stage in range(7):
        for one in flows:
            next(one)
        if stage == 0:
            send_all(slab, tile, (send, recv), -1, halo, coming)
        if stage == 1:
            wait_all(slab, tile, (send, recv), -1, halo, coming)
            blocks = grad.shape[0]
            back = coming[...].reshape(-1, coming.shape[-1])
            for n in range(blocks):
                grad[n] = base[n] + dot(hot(BLOCK, lists[...] - n * BLOCK), back)
    total[...] = result[...]


def body(features, conv_weight, down_weight, coarse_grad, rulebook, boundary_rows, parent_code):
    rows, chans = features.shape
    coarse_rows, out_chans = coarse_grad.shape
    list_len = boundary_rows.shape[1]
    childs = down_weight.shape[0]
    kernels = conv_weight.shape[0]
    blocks = rows // BLOCK
    per_list = list_len // BLOCK
    total_blocks = blocks + 4 * per_list
    slab, tile = lax.axis_size("slab"), lax.axis_size("tile")
    high_count = tile // 2
    used = (kernels + childs) * BLOCK
    chunk = -(-used // (16 * slab * tile)) * 16
    vmem = pl.BlockSpec(memory_space=pltpu.VMEM)
    lists = boundary_rows.reshape(1, 4 * list_len)

    table = pl.pallas_call(
        functools.partial(halo_kernel, slab, tile),
        out_shape=jax.ShapeDtypeStruct((total_blocks, chans, BLOCK), BF16),
        in_specs=[vmem] * 2,
        out_specs=vmem,
        scratch_shapes=[
            pltpu.VMEM((4, per_list, chans, BLOCK), BF16),
            pltpu.VMEM((4, per_list, chans, BLOCK), BF16),
            pltpu.SemaphoreType.DMA((4,)),
            pltpu.SemaphoreType.DMA((4,)),
        ],
        compiler_params=pltpu.CompilerParams(
            collective_id=0, has_side_effects=True, vmem_limit_bytes=32 * 2**20
        ),
        name="halo",
    )(features.reshape(blocks, BLOCK, chans), lists)
    wflat = conv_weight.transpose(2, 0, 1).reshape(out_chans, kernels * chans)
    book = rulebook.reshape(kernels, blocks, BLOCK)
    src = jnp.minimum(jnp.min(book, axis=2) // BLOCK, total_blocks - 1)
    coarse, part, local_grad, halo_grad = pl.pallas_call(
        main_kernel,
        out_shape=(
            jax.ShapeDtypeStruct((coarse_rows, out_chans), BF16),
            jax.ShapeDtypeStruct((chunk * slab * tile, out_chans), BF16),
            jax.ShapeDtypeStruct((blocks, BLOCK, chans), F32),
            jax.ShapeDtypeStruct((4, list_len, chans), BF16),
        ),
        in_specs=[pl.BlockSpec(memory_space=pltpu.SMEM)] + [vmem] * 7,
        out_specs=(vmem,) * 4,
        scratch_shapes=[
            pltpu.VMEM((total_blocks, BLOCK, chans), F32),
            pltpu.VMEM((kernels * BLOCK, 2 * BLOCK), BF16),
            pltpu.VMEM((blocks // 2, 2 * BLOCK, 2 * chans), BF16),
            pltpu.VMEM((GROUP, blocks // 2, BLOCK, 2 * chans), BF16),
            pltpu.VMEM((childs, blocks, coarse_rows // blocks, chans), BF16),
            pltpu.VMEM((childs, blocks, coarse_rows // blocks, chans), BF16),
        ],
        compiler_params=pltpu.CompilerParams(vmem_limit_bytes=40 * 2**20),
        name="sparse_conv",
    )(
        src, table, wflat, conv_weight, down_weight, coarse_grad, book,
        parent_code.reshape(blocks, BLOCK),
    )

    def landings(piece, outer, inner):
        wide = inner * piece
        shapes = [(outer * wide,), (outer * wide,), (outer - 1, wide), (wide,), (inner - 1, piece)]
        return [pltpu.VMEM(shape + (out_chans,), BF16) for shape in shapes]

    first_piece = -(-chunk * 2 // 48) * 16
    pieces = (first_piece, chunk - first_piece)
    copies = 4 + 4 * (1 + (slab - 1) + (high_count - 1))
    total, input_grad = pl.pallas_call(
        functools.partial(reduce_kernel, slab, tile, pieces),
        out_shape=(
            jax.ShapeDtypeStruct(part.shape, BF16),
            jax.ShapeDtypeStruct((blocks, BLOCK, chans), F32),
        ),
        in_specs=[vmem] * 4,
        out_specs=(vmem,) * 2,
        scratch_shapes=[
            pltpu.VMEM(part.shape, BF16),
            pltpu.VMEM((4, list_len, chans), BF16),
            pltpu.SemaphoreType.DMA((copies,)),
            pltpu.SemaphoreType.DMA((copies,)),
        ]
        + landings(pieces[0], slab, high_count)
        + landings(pieces[1], high_count, slab),
        compiler_params=pltpu.CompilerParams(
            collective_id=1, has_side_effects=True, vmem_limit_bytes=32 * 2**20
        ),
        name="reduce",
    )(part, halo_grad, local_grad, lists)
    total = total.astype(F32)
    conv_grad = total[: kernels * BLOCK].reshape(conv_weight.shape)
    down_grad = total[kernels * BLOCK : used].reshape(down_weight.shape)
    return (coarse, input_grad.reshape(rows, chans), conv_grad, down_grad)


def solution(mesh):
    return jax.shard_map(
        body,
        mesh=mesh,
        in_specs=(
            P(("slab", "tile"), None),
            P(),
            P(),
            P(("slab", "tile"), None),
            P(None, ("slab", "tile")),
            P(("slab", "tile"), None),
            P(("slab", "tile")),
        ),
        out_specs=(P(("slab", "tile"), None), P(("slab", "tile"), None), P(), P()),
        check_vma=False,
    )
```

```python
import functools

import jax
import jax.numpy as jnp
from jax import lax
from jax.experimental import pallas as pl
from jax.experimental.pallas import tpu as pltpu
from jax.sharding import PartitionSpec as P

BLOCK = 128
GROUP = 3
F32 = jnp.float32
BF16 = jnp.bfloat16
LAST = (((1,), (1,)), ((), ()))
FIRST = (((0,), (0,)), ((), ()))
MESH = pl.DeviceIdType.MESH


def dot(a, b):
    return jnp.dot(a, b, preferred_element_type=F32)


def hot(rows, index):
    short = jnp.clip(index, -1, rows).astype(jnp.int16)
    same = lax.broadcasted_iota(jnp.int16, (rows, index.shape[1]), 0) == short
    return jnp.where(same, jnp.ones((), BF16), jnp.zeros((), BF16))


def diagonal(first, second):
    empty = jnp.zeros_like(first)
    top = jnp.concatenate([first, empty], axis=1)
    return jnp.concatenate([top, jnp.concatenate([empty, second], axis=1)], axis=0)


def main_kernel(
    src, table, wflat, weight, down, cgrad, book, code,
    coarse, part, local_grad, halo_grad,
    ext_grad, gathered, pre_grad, sums, spread, children,
):
    kernels, blocks = src.shape
    childs, _, quarter, chans = spread.shape
    pairs = blocks // 2
    group = sums.shape[0]
    ext_grad[...] = jnp.zeros_like(ext_grad)
    children[...] = jnp.zeros_like(children)
    for s in range(childs):
        one = lax.dot_general(cgrad[...], down[s], LAST, preferred_element_type=F32)
        spread[s] = one.astype(BF16).reshape(blocks, quarter, chans)

    def pick(k, b):
        return hot(BLOCK, book[b, pl.ds(k, 1), :] - src[k, b] * BLOCK)

    def pair_of(k, p):
        return jnp.concatenate([table[src[k, 2 * p]], table[src[k, 2 * p + 1]]], axis=1)

    def forward(p, carry):
        for k in range(kernels):
            got = dot(pair_of(k, p), diagonal(pick(k, 2 * p), pick(k, 2 * p + 1)))
            gathered[k * BLOCK : (k + 1) * BLOCK, :] = got.astype(BF16)
        pre_both = dot(wflat[...], gathered[...])
        grads = []
        for i in range(2):
            b = 2 * p + i
            pre = pre_both[:, i * BLOCK : (i + 1) * BLOCK].T
            hidden = jnp.maximum(pre, 0.0).astype(BF16)
            own = code[pl.ds(b, 1), :]
            place = (own % childs) * quarter + (own // childs - b * quarter)
            place = jnp.where(own // childs < blocks * quarter, place, -1)
            family = hot(childs * quarter, place)
            kids = dot(family, hidden).astype(BF16)
            children[:, b] = kids.reshape(childs, quarter, chans)
            share = spread[:, b].reshape(childs * quarter, chans)
            back = lax.dot_general(family, share, FIRST, preferred_element_type=F32)
            grads.append(jnp.where(pre > 0, back, 0.0).astype(BF16))
        pre_grad[p] = diagonal(*grads)
        return carry

    lax.fori_loop(0, pairs, forward, 0)

    coarse_total = jnp.zeros(coarse.shape, F32)
    for s in range(childs):
        kids = children[s].reshape(blocks * quarter, chans)
        coarse_total += dot(kids, down[s])
        one = lax.dot_general(kids, cgrad[...], FIRST, preferred_element_type=F32)
        part[(kernels + s) * BLOCK : (kernels + s + 1) * BLOCK, :] = one.astype(BF16)
    coarse[...] = coarse_total.astype(BF16)
    used = (kernels + childs) * BLOCK
    if used < part.shape[0]:
        part[used:, :] = jnp.zeros((part.shape[0] - used, part.shape[1]), BF16)

    def backward(step, carry):
        first = step * group
        for p in range(pairs):
            picks = [
                jnp.concatenate([pick(first + g, 2 * p), pick(first + g, 2 * p + 1)], axis=1)
                for g in range(group)
            ]
            both = dot(jnp.concatenate(picks, axis=0), pre_grad[p]).astype(BF16)
            for g in range(group):
                sums[g, p] = both[g * BLOCK : (g + 1) * BLOCK]
        for g in range(group):
            k = first + g
            twice = diagonal(weight[k], weight[k])
            total = jnp.zeros(weight.shape[1:], F32)
            for p in range(pairs):
                both = sums[g, p]
                terms = lax.dot_general(both, twice, LAST, preferred_element_type=F32)
                stacked = jnp.concatenate([both[:, :BLOCK], both[:, BLOCK:]], axis=0)
                total += dot(pair_of(k, p), stacked)
                for i in range(2):
                    ext_grad[src[k, 2 * p + i]] += terms[:, i * BLOCK : (i + 1) * BLOCK]
            part[pl.ds(pl.multiple_of(k * BLOCK, BLOCK), BLOCK), :] = total.astype(BF16)
        return carry

    lax.fori_loop(0, kernels // group, backward, 0)
    local_grad[...] = ext_grad[:blocks]
    halo_grad[...] = ext_grad[blocks:].reshape(halo_grad.shape).astype(BF16)


def exchange(slab, tile, sems, base):
    me_s, me_t = lax.axis_index("slab"), lax.axis_index("tile")
    steps = ((1, 0), (-1, 0), (0, 1), (0, -1))

    def there(ds, dt):
        s, t = me_s + ds, me_t + dt
        return (s >= 0) & (s < slab) & (t >= 0) & (t < tile)

    def make(d, sign, src, dst):
        ds, dt = steps[d][0] * sign, steps[d][1] * sign
        to = (lax.rem(me_s + ds + slab, slab), lax.rem(me_t + dt + tile, tile))
        send, recv = sems
        return pltpu.make_async_remote_copy(
            src_ref=src, dst_ref=dst, send_sem=send.at[base + d], recv_sem=recv.at[base + d],
            device_id=to, device_id_type=MESH,
        )

    return steps, there, make


def greet_neighbours(slab, tile, barrier):
    me_s, me_t = lax.axis_index("slab"), lax.axis_index("tile")
    steps, there, _ = exchange(slab, tile, None, 0)
    for ds, dt in steps:

        @pl.when(there(ds, dt))
        def _(ds=ds, dt=dt):
            pl.semaphore_signal(
                barrier, inc=1, device_id=(me_s + ds, me_t + dt), device_id_type=MESH
            )


def neighbour_count(slab, tile):
    steps, there, _ = exchange(slab, tile, None, 0)
    return sum(jnp.where(there(ds, dt), 1, 0) for ds, dt in steps)


def send_all(slab, tile, sems, sign, src, dst):
    steps, there, make = exchange(slab, tile, sems, 0)
    for d, (ds, dt) in enumerate(steps):

        @pl.when(there(ds * sign, dt * sign))
        def _(d=d):
            make(d, sign, src.at[d], dst.at[d]).start()


def wait_all(slab, tile, sems, sign, src, dst):
    steps, there, make = exchange(slab, tile, sems, 0)
    for d, (ds, dt) in enumerate(steps):

        @pl.when(there(ds * sign, dt * sign))
        def _(d=d):
            make(d, sign, src.at[d], dst.at[d]).wait_send()

        @pl.when(there(-ds * sign, -dt * sign))
        def _(d=d):
            make(d, sign, src.at[d], dst.at[d]).wait_recv()


def halo_kernel(slab, tile, features, lists, weight, book, table, wflat, source, split, outgoing, arrived, send, recv):
    blocks = features.shape[0]
    per_list = outgoing.shape[1]
    arrived[...] = jnp.zeros_like(arrived)
    barrier = pltpu.get_barrier_semaphore()
    greet_neighbours(slab, tile, barrier)
    for n in range(blocks):
        table[n] = features[n].astype(F32).T.astype(BF16)
    local = jnp.concatenate([table[n] for n in range(blocks)], axis=1)
    width = per_list * BLOCK
    for d in range(4):
        rows = hot(blocks * BLOCK, lists[:, d * width : (d + 1) * width])
        picked = dot(local, rows).astype(BF16)
        for j in range(per_list):
            outgoing[d, j] = picked[:, j * BLOCK : (j + 1) * BLOCK]
    pl.semaphore_wait(barrier, neighbour_count(slab, tile))
    send_all(slab, tile, (send, recv), 1, outgoing, arrived)
    kernels = weight.shape[0]
    for k in range(kernels):
        wflat[:, k * BLOCK : (k + 1) * BLOCK] = weight[k].astype(F32).T.astype(BF16)
    columns = lax.broadcasted_iota(jnp.int32, source.shape, 1)
    lowest = jnp.zeros(source.shape, F32)
    for n in range(blocks):
        own = book[:, n * BLOCK : (n + 1) * BLOCK]
        split[n] = own
        one = own.astype(F32)
        lowest = jnp.where(columns == n, jnp.min(one, axis=1, keepdims=True), lowest)
    source[...] = jnp.minimum(lowest.astype(jnp.int32) >> 7, table.shape[0] - 1)
    wait_all(slab, tile, (send, recv), 1, outgoing, arrived)
    for d in range(4):
        for j in range(per_list):
            table[blocks + d * per_list + j] = arrived[d, j]


def reduce_kernel(slab, tile, pieces, part, halo, base, lists, total, grad, result, coming, send, recv, *buffers):
    high_count = tile // 2
    me_s, me_t = lax.axis_index("slab"), lax.axis_index("tile")
    core, high = lax.rem(me_t, 2), lax.div(me_t, 2)
    pair = me_t + 1 - 2 * core

    def rows(start, count):
        return pl.ds(pl.multiple_of(start, 16), count)

    def remote(src, dst, i, to):
        return pltpu.make_async_remote_copy(
            src_ref=src, dst_ref=dst, send_sem=send.at[i], recv_sem=recv.at[i],
            device_id=to, device_id_type=MESH,
        )

    slab_peers = [lax.rem(me_s + d, slab) for d in range(1, slab)]
    high_peers = [lax.rem(high + d, high_count) for d in range(1, high_count)]
    along_slab = (slab, me_s, [(s, (s, me_t)) for s in slab_peers])
    along_high = (high_count, high, [(h, (me_s, h * 2 + core)) for h in high_peers])
    one_way = 1 + len(slab_peers) + len(high_peers)

    def flow(start, piece, outer, inner, at, from_pair, after_pair, from_outer, after_outer, from_inner):
        outer_count, outer_me, outer_peers = outer
        inner_count, inner_me, inner_peers = inner
        wide = inner_count * piece
        half = outer_count * wide

        def scatter(held, size, landing, peers, at):
            copies = []
            for d, (index, to) in enumerate(peers):
                copies.append(remote(held.at[rows(index * size, size)], landing.at[d], at + d, to))
                copies[-1].start()
            return copies

        def share(first_row, count, devices, at):
            where = rows(first_row, count)
            copies = [remote(result.at[where], result.at[where], at + d, to) for d, to in enumerate(devices)]
            for copy in copies:
                copy.start()
            return copies

        def wait(copies):
            for copy in copies:
                copy.wait()

        def summed(held, size, me, landing, peers):
            mine = held[rows(me * size, size), :].astype(F32)
            for d in range(len(peers)):
                mine += landing[d].astype(F32)
            return mine.astype(BF16)

        first = remote(part.at[rows(start + (1 - core) * half, half)], from_pair, at, (me_s, pair))
        first.start()
        yield
        first.wait()
        mine = part[rows(start + core * half, half), :].astype(F32) + from_pair[...].astype(F32)
        after_pair[...] = mine.astype(BF16)
        copies = scatter(after_pair, wide, from_outer, outer_peers, at + 1)
        yield
        wait(copies)
        after_outer[...] = summed(after_pair, wide, outer_me, from_outer, outer_peers)
        copies = scatter(after_outer, piece, from_inner, inner_peers, at + 1 + len(outer_peers))
        yield
        wait(copies)
        own_half = start + core * half
        own_wide = own_half + outer_me * wide
        own = own_wide + inner_me * piece
        result[rows(own, piece), :] = summed(after_outer, piece, inner_me, from_inner, inner_peers)
        at += one_way
        copies = share(own, piece, [to for _, to in inner_peers], at)
        yield
        wait(copies)
        copies = share(own_wide, wide, [to for _, to in outer_peers], at + len(inner_peers))
        yield
        wait(copies)
        copies = share(own_half, half, [(me_s, pair)], at + one_way - 1)
        yield
        wait(copies)
        yield

    coming[...] = jnp.zeros_like(coming)
    barrier = pltpu.get_barrier_semaphore()
    greeted = [(me_s, pair)] + [to for _, to in along_slab[2]] + [to for _, to in along_high[2]]
    for to in greeted:
        pl.semaphore_signal(barrier, inc=1, device_id=to, device_id_type=MESH)
    beside = me_t + 2 * core - 1
    has_beside = (beside >= 0) & (beside < tile)

    @pl.when(has_beside)
    def _():
        pl.semaphore_signal(barrier, inc=1, device_id=(me_s, beside), device_id_type=MESH)

    pl.semaphore_wait(barrier, len(greeted) + jnp.where(has_beside, 1, 0))

    count = len(buffers) // 2
    flows = [
        flow(0, pieces[0], along_slab, along_high, 4, *buffers[:count]),
        flow(pieces[0] * slab * tile, pieces[1], along_high, along_slab, 4 + 2 * one_way, *buffers[count:]),
    ]
    for stage in range(7):
        for one in flows:
            next(one)
        if stage == 0:
            send_all(slab, tile, (send, recv), -1, halo, coming)
        if stage == 1:
            wait_all(slab, tile, (send, recv), -1, halo, coming)
            blocks = grad.shape[0]
            back = coming[...].reshape(-1, coming.shape[-1])
            for n in range(blocks):
                grad[n] = base[n] + dot(hot(BLOCK, lists[...] - n * BLOCK), back)
    total[...] = result[...]


def body(features, conv_weight, down_weight, coarse_grad, rulebook, boundary_rows, parent_code):
    rows, chans = features.shape
    coarse_rows, out_chans = coarse_grad.shape
    list_len = boundary_rows.shape[1]
    childs = down_weight.shape[0]
    kernels = conv_weight.shape[0]
    blocks = rows // BLOCK
    per_list = list_len // BLOCK
    total_blocks = blocks + 4 * per_list
    slab, tile = lax.axis_size("slab"), lax.axis_size("tile")
    high_count = tile // 2
    used = (kernels + childs) * BLOCK
    chunk = -(-used // (16 * slab * tile)) * 16
    vmem = pl.BlockSpec(memory_space=pltpu.VMEM)
    lists = boundary_rows.reshape(1, 4 * list_len)

    table, wflat, src, book = pl.pallas_call(
        functools.partial(halo_kernel, slab, tile),
        out_shape=(
            jax.ShapeDtypeStruct((total_blocks, chans, BLOCK), BF16),
            jax.ShapeDtypeStruct((out_chans, kernels * chans), BF16),
            jax.ShapeDtypeStruct((kernels, blocks), jnp.int32),
            jax.ShapeDtypeStruct((blocks, kernels, BLOCK), jnp.int32),
        ),
        in_specs=[vmem] * 4,
        out_specs=(vmem,) * 4,
        scratch_shapes=[
            pltpu.VMEM((4, per_list, chans, BLOCK), BF16),
            pltpu.VMEM((4, per_list, chans, BLOCK), BF16),
            pltpu.SemaphoreType.DMA((4,)),
            pltpu.SemaphoreType.DMA((4,)),
        ],
        compiler_params=pltpu.CompilerParams(
            collective_id=0, has_side_effects=True, vmem_limit_bytes=32 * 2**20
        ),
        name="halo",
    )(features.reshape(blocks, BLOCK, chans), lists, conv_weight, rulebook)
    coarse, part, local_grad, halo_grad = pl.pallas_call(
        main_kernel,
        out_shape=(
            jax.ShapeDtypeStruct((coarse_rows, out_chans), BF16),
            jax.ShapeDtypeStruct((chunk * slab * tile, out_chans), BF16),
            jax.ShapeDtypeStruct((blocks, BLOCK, chans), F32),
            jax.ShapeDtypeStruct((4, list_len, chans), BF16),
        ),
        in_specs=[pl.BlockSpec(memory_space=pltpu.SMEM)] + [vmem] * 7,
        out_specs=(vmem,) * 4,
        scratch_shapes=[
            pltpu.VMEM((total_blocks, BLOCK, chans), F32),
            pltpu.VMEM((kernels * BLOCK, 2 * BLOCK), BF16),
            pltpu.VMEM((blocks // 2, 2 * BLOCK, 2 * chans), BF16),
            pltpu.VMEM((GROUP, blocks // 2, BLOCK, 2 * chans), BF16),
            pltpu.VMEM((childs, blocks, coarse_rows // blocks, chans), BF16),
            pltpu.VMEM((childs, blocks, coarse_rows // blocks, chans), BF16),
        ],
        compiler_params=pltpu.CompilerParams(vmem_limit_bytes=40 * 2**20),
        name="sparse_conv",
    )(
        src, table, wflat, conv_weight, down_weight, coarse_grad, book,
        parent_code.reshape(blocks, BLOCK),
    )

    def landings(piece, outer, inner):
        wide = inner * piece
        shapes = [(outer * wide,), (outer * wide,), (outer - 1, wide), (wide,), (inner - 1, piece)]
        return [pltpu.VMEM(shape + (out_chans,), BF16) for shape in shapes]

    first_piece = -(-chunk * 2 // 48) * 16
    pieces = (first_piece, chunk - first_piece)
    copies = 4 + 4 * (1 + (slab - 1) + (high_count - 1))
    total, input_grad = pl.pallas_call(
        functools.partial(reduce_kernel, slab, tile, pieces),
        out_shape=(
            jax.ShapeDtypeStruct(part.shape, BF16),
            jax.ShapeDtypeStruct((blocks, BLOCK, chans), F32),
        ),
        in_specs=[vmem] * 4,
        out_specs=(vmem,) * 2,
        scratch_shapes=[
            pltpu.VMEM(part.shape, BF16),
            pltpu.VMEM((4, list_len, chans), BF16),
            pltpu.SemaphoreType.DMA((copies,)),
            pltpu.SemaphoreType.DMA((copies,)),
        ]
        + landings(pieces[0], slab, high_count)
        + landings(pieces[1], high_count, slab),
        compiler_params=pltpu.CompilerParams(
            collective_id=1, has_side_effects=True, vmem_limit_bytes=32 * 2**20
        ),
        name="reduce",
    )(part, halo_grad, local_grad, lists)
    total = total.astype(F32)
    conv_grad = total[: kernels * BLOCK].reshape(conv_weight.shape)
    down_grad = total[kernels * BLOCK : used].reshape(down_weight.shape)
    return (coarse, input_grad.reshape(rows, chans), conv_grad, down_grad)


def solution(mesh):
    return jax.shard_map(
        body,
        mesh=mesh,
        in_specs=(
            P(("slab", "tile"), None),
            P(),
            P(),
            P(("slab", "tile"), None),
            P(None, ("slab", "tile")),
            P(("slab", "tile"), None),
            P(("slab", "tile")),
        ),
        out_specs=(P(("slab", "tile"), None), P(("slab", "tile"), None), P(), P()),
        check_vma=False,
    )
```
